32 devices in a mesh: groups: 2 (over y), row: 4 (over z), col: 2 (over x), rep: 2 (over core).
Axes of the slice: x: 2, y: 2, z: 4, core: 2. Of those that a mesh axis runs over, the one named last changes fastest.
Arguments:
- sep_inverse: float32 [6144, 3072], P(('groups', 'row'), ('col', 'rep')), parts along dimension 0, may hold values from -6 to 6
- row_tiles: int32 [12], replicated, may hold values from 0 to 23, as said below
- panel_rows: float32 [3072, 512], P(('groups', 'row')), parts along dimension 0, may hold values from -0.15625 to 0.15625
- diag_inverse: float32 [1024, 512], P('groups'), parts along dimension 0, as said below
Outputs:
- sigma_rows: float32 [3072, 512], P(('groups', 'row', 'col', 'rep')), parts along dimension 0
- sigma_diag: float32 [1024, 512], P(('groups', 'col', 'rep')), parts along dimension 0
- variances: float32 [1024], P(('groups', 'col', 'rep')), parts along dimension 0
The draws below stay inside these ranges and needn't reach their ends.
There are 2 independent parts, one for each index of `groups`. The reference program is written for one: setup_inputs(seed, part) draws one part's arguments, and reference() takes and returns one part's arrays. A program takes and returns all parts, laid end to end along the dimension named above; an argument that names none is the same for every part. Nothing has to cross between parts.
Inputs may be any that keep to these rules, and one draw needn't show every extreme that they name: row_tiles holds, for each aligned block of 6 separator tiles, 3 distinct tiles of that block in increasing order; slot k lies in block k // 3. diag_inverse is lower triangular with a positive diagonal.
All inputs are finite; a program needn't handle non-finite values.
Results may differ from the reference program's by a relative error of at most 0.000071.
Values sent between devices are 32-bit elements; how exact they have to be, the bound alone decides.
No kernel may reach another device: no remote copies, remote signals or barrier semaphores. Data moves between devices by JAX's collectives and lax.ppermute only.
A program may use at most 64 MiB of HBM per device.

```python
import math
import jax
import jax.numpy as jnp
from jax import lax

TILE = 128
PANEL = 512
BLOCK_SLOTS = 3
BLOCK_TILES = 6
SEP_TILES = 24
SEP = 3072
PANEL_ROWS = 1536


def draw_row_tiles(key, part):
    key = jax.random.fold_in(key, 11)
    blocks = SEP_TILES // BLOCK_TILES
    subkeys = jax.random.split(key, blocks)
    block_ids = jnp.arange(blocks, dtype=jnp.int32)
    force_low = block_ids == 0
    force_high = block_ids == blocks - 1

    def choose(subkey, low_flag, high_flag):
        order = jax.random.permutation(subkey, BLOCK_TILES).astype(jnp.int32)
        ranks = jnp.argsort(order).astype(jnp.int32)
        positions = jnp.arange(BLOCK_TILES, dtype=jnp.int32)
        forced = (positions == 0) & low_flag | (positions == BLOCK_TILES - 1) & high_flag
        priority = jnp.where(forced, -1, ranks).astype(jnp.int32)
        picked = jnp.argsort(priority, stable=True)[:BLOCK_SLOTS].astype(jnp.int32)
        return jnp.sort(picked)
    chosen = jax.vmap(choose)(subkeys, force_low, force_high).astype(jnp.int32)
    starts = block_ids[:, None] * BLOCK_TILES
    return (chosen + starts).reshape(-1).astype(jnp.int32)


def draw_diag_inverse(key, part):
    key = jax.random.fold_in(key, 23)
    first_key, second_key = jax.random.split(key)
    lower = jax.random.normal(first_key, (PANEL, PANEL), jnp.float32) / math.sqrt(PANEL)
    diagonal = jax.random.uniform(second_key, (PANEL,), jnp.float32, 0.5, 1.5)
    return jnp.tril(lower, -1) + jnp.diag(diagonal)


def strengthened(array, stream_key, source, target, parts, factor):
    owner, partner = [(jnp.arange(array.shape[position]) // (array.shape[position] // parts)).reshape([-1 if axis == position else 1 for axis in range(array.ndim)]) for position in (source, target)]
    chosen = jax.random.permutation(stream_key, parts)[partner]
    strong = (owner == chosen) | (owner == (partner + parts // 2) % parts)
    return jnp.where(strong, factor * array, array)


def block_levels(stream_key, shape, pieces, smallest, high):
    gain, own = 1.0, jax.random.fold_in(stream_key, 6)
    for axis_at, shards_of in pieces:
        draws = jnp.exp(jax.random.uniform(jax.random.fold_in(own, axis_at), (shards_of,), jnp.float32, smallest / len(pieces), high / len(pieces)))
        gain = gain * jnp.repeat(draws, shape[axis_at] // shards_of).reshape([-1 if axis == axis_at else 1 for axis in range(len(shape))])
    return gain


def normal_values(own_key, shape, deviation, limit, pieces=(), kind=jnp.bfloat16):
    values = deviation * jax.random.normal(own_key, shape, jnp.float32)
    if pieces:
        values = values * block_levels(own_key, shape, pieces, -0.22, 0.18)
    return jnp.clip(values, -limit, limit).astype(kind)


def noise_with(stream_key, extent, scale, reach, cuts, heavy, held_as=jnp.bfloat16):
    values = scale * jax.random.normal(stream_key, extent, jnp.float32)
    if cuts:
        values = values * block_levels(stream_key, extent, cuts, -0.22, 0.18)
    return jnp.clip(strengthened(values, jax.random.fold_in(stream_key, 3), *heavy), -reach, reach).astype(held_as)


def setup_inputs(seed: int = 0, part: int = 0) -> dict:
    keys = jax.random.split(jax.random.key(seed), 5)
    part_keys = jax.random.split(jax.random.fold_in(keys[4], part), 5)
    sep_inverse = noise_with(part_keys[0], (SEP, SEP), 1.0, 6.0, ((0, 4), (1, 4)), (1, 0, 4, 2.0), jnp.float32)
    row_tiles = draw_row_tiles(jax.random.fold_in(keys[4], 71), part)
    panel_rows = normal_values(part_keys[2], (PANEL_ROWS, PANEL), PANEL_ROWS ** -0.5, 0.15625, ((0, 4),), jnp.float32)
    diag_inverse = draw_diag_inverse(jax.random.fold_in(jax.random.fold_in(keys[4], part), 71), part)
    return dict(sep_inverse=sep_inverse, row_tiles=row_tiles, panel_rows=panel_rows, diag_inverse=diag_inverse)


def reference(sep_inverse, row_tiles, panel_rows, diag_inverse):
    highest = lax.Precision.HIGHEST
    offsets = jnp.arange(TILE, dtype=jnp.int32)
    index = (row_tiles[:, None].astype(jnp.int32) * TILE + offsets[None, :]).reshape(-1).astype(jnp.int32)
    sep_block = jnp.take(jnp.take(sep_inverse, index, axis=0), index, axis=1)
    whitened = jnp.dot(panel_rows, diag_inverse, precision=highest, preferred_element_type=jnp.float32)
    sigma_rows = -jnp.dot(sep_block, whitened, precision=highest, preferred_element_type=jnp.float32)
    inner = jnp.dot(diag_inverse.T, diag_inverse, precision=highest, preferred_element_type=jnp.float32)
    correction = jnp.dot(sigma_rows.T, whitened, precision=highest, preferred_element_type=jnp.float32)
    sigma_diag = inner - correction
    variances = jnp.diagonal(sigma_diag)
    return sigma_rows, sigma_diag, variances
```

```python
import jax
import jax.numpy as jnp
from jax import lax
from jax.experimental import pallas as pl
from jax.experimental.pallas import tpu as pltpu
from jax.sharding import PartitionSpec as P

TILE = 128
VMEM = pl.BlockSpec(memory_space=pltpu.VMEM)
SMEM = pl.BlockSpec(memory_space=pltpu.SMEM)
ANY = pl.BlockSpec(memory_space=pl.ANY)
PARAMS = pltpu.CompilerParams(vmem_limit_bytes=32 * 1024 * 1024)


def broadcast(x, axis, root):
    mine = lax.axis_index(axis) == root
    return lax.psum(jnp.where(mine, x, jnp.zeros_like(x)), axis)


def contract_rows(left, right):
    return lax.dot_general(
        left,
        right,
        (((0,), (0,)), ((), ())),
        precision=lax.Precision.HIGHEST,
        preferred_element_type=jnp.float32,
    )


def any_mesh(sep_inverse, row_tiles, panel_rows, diag_inverse):
    highest = lax.Precision.HIGHEST
    members = lax.axis_size(("col", "rep"))
    column_index = lax.axis_index(("col", "rep"))
    row_index = lax.axis_index("row")
    block_slots = panel_rows.shape[0] // TILE
    block_tiles = sep_inverse.shape[0] // TILE
    width = panel_rows.shape[1]
    own_tiles = (
        lax.dynamic_slice_in_dim(row_tiles, row_index * block_slots, block_slots)
        - row_index * block_tiles
    )
    far_tiles = (
        lax.dynamic_slice_in_dim(row_tiles, column_index * block_slots, block_slots)
        - column_index * block_tiles
    )
    tiled = sep_inverse.reshape(block_tiles, TILE, block_tiles, TILE)
    picked = jnp.take(jnp.take(tiled, own_tiles, axis=0), far_tiles, axis=2)
    picked = picked.reshape(block_slots * TILE, block_slots * TILE)
    own_white = jnp.dot(
        panel_rows, diag_inverse, precision=highest, preferred_element_type=jnp.float32
    )
    far_white = broadcast(own_white, "row", column_index)
    partial_value = -jnp.dot(
        picked, far_white, precision=highest, preferred_element_type=jnp.float32
    )
    piece = partial_value.shape[0] // members
    count = width // members
    first = column_index * count
    sigma_rows = lax.psum_scatter(partial_value, ("col", "rep"), scatter_dimension=0, tiled=True)
    white_mine = lax.dynamic_slice_in_dim(own_white, column_index * piece, piece, 0)
    local_block = lax.psum_scatter(
        contract_rows(sigma_rows, white_mine), ("col", "rep"), scatter_dimension=0, tiled=True
    )
    summed = lax.psum(local_block, "row")
    inverse_cols = lax.dynamic_slice_in_dim(diag_inverse, first, count, 1)
    sigma_diag = contract_rows(inverse_cols, diag_inverse) - summed
    variances = jnp.diagonal(lax.dynamic_slice_in_dim(sigma_diag, first, count, 1))
    return (sigma_rows, sigma_diag, variances)


def split(x):
    high = x.astype(jnp.bfloat16)
    return high, (x - high.astype(jnp.float32)).astype(jnp.bfloat16)


def dot(a, b):
    return jnp.dot(a, b, preferred_element_type=jnp.float32)


def dot3(a, b):
    return dot(a[0], b[0]) + (dot(a[0], b[1]) + dot(a[1], b[0]))


def f32(*shape):
    return jax.ShapeDtypeStruct(shape, jnp.float32)


def pick_kernel(tiles_ref, sep_ref, out_ref, sems):
    row, member = lax.axis_index("row"), lax.axis_index(("col", "rep"))
    slots, block = out_ref.shape[0] // TILE, sep_ref.shape[0] // TILE
    copies = []
    for i in range(slots):
        down = (tiles_ref[row * slots + i] - row * block) * TILE
        for j in range(slots):
            across = (tiles_ref[member * slots + j] - member * block) * TILE
            copies.append(
                pltpu.make_async_copy(
                    sep_ref.at[
                        pl.ds(pl.multiple_of(down, TILE), TILE),
                        pl.ds(pl.multiple_of(across, TILE), TILE),
                    ],
                    out_ref.at[pl.ds(i * TILE, TILE), pl.ds(j * TILE, TILE)],
                    sems.at[i * slots + j],
                )
            )
    for copy in copies:
        copy.start()
    for copy in copies:
        copy.wait()


def pick(row_tiles, sep_inverse, slots):
    return pl.pallas_call(
        pick_kernel,
        out_shape=f32(slots * TILE, slots * TILE),
        in_specs=[SMEM, ANY],
        out_specs=ANY,
        scratch_shapes=[pltpu.SemaphoreType.DMA((slots * slots,))],
        compiler_params=PARAMS,
    )(row_tiles, sep_inverse)


def quarter_kernel(panel_ref, inverse_ref, out_ref):
    member = lax.axis_index(("col", "rep"))
    columns = pl.ds(pl.multiple_of(member * TILE, TILE), TILE)
    out_ref[...] = dot3(split(panel_ref[...]), split(inverse_ref[:, columns]))


def white_quarter(panel_rows, diag_inverse):
    return pl.pallas_call(
        quarter_kernel,
        out_shape=f32(panel_rows.shape[0], TILE),
        in_specs=[VMEM, VMEM],
        out_specs=VMEM,
        compiler_params=PARAMS,
    )(panel_rows, diag_inverse)


def whiten_kernel(panel_ref, inverse_ref, high_ref, low_ref, base_ref):
    member = lax.axis_index(("col", "rep"))
    columns = pl.ds(pl.multiple_of(member * TILE, TILE), TILE)
    inverse = split(inverse_ref[...])
    high, low = split(dot3(split(panel_ref[...]), inverse))
    high_ref[...] = high
    low_ref[...] = low
    base_ref[...] = dot3(split(inverse_ref[:, columns].T), inverse)


def whiten(panel_rows, diag_inverse):
    shape = jax.ShapeDtypeStruct(panel_rows.shape, jnp.bfloat16)
    return pl.pallas_call(
        whiten_kernel,
        out_shape=(shape, shape, f32(TILE, diag_inverse.shape[1])),
        in_specs=[VMEM, VMEM],
        out_specs=(VMEM,) * 3,
        compiler_params=PARAMS,
    )(panel_rows, diag_inverse)


def product_kernel(*refs):
    seps, whites, (own_high, own_low) = refs[0:4], refs[4:8], refs[8:10]
    terms, pieces = refs[10:14], refs[14:18]
    white_high, white_low, product = refs[18:21]
    row, member = lax.axis_index("row"), lax.axis_index(("col", "rep"))
    for j in range(4):
        high, low = split(whites[j][...])
        white_high[row ^ j] = high
        white_low[row ^ j] = low
    total = None
    for i in range(4):
        term = dot3(split(seps[i][...]), (white_high[member ^ i], white_low[member ^ i]))
        total = term if total is None else total + term
    product[...] = -total
    flipped = split(total.T)
    count = pieces[0].shape[0]
    for j in range(4):
        columns = pl.ds(pl.multiple_of((row ^ j) * TILE, TILE), TILE)
        terms[j][...] = dot3(flipped, (own_high[:, columns], own_low[:, columns]))
        pieces[j][...] = product[pl.ds(pl.multiple_of((member ^ j) * count, 8), count), :]


def products(seps, whites, own_white):
    depth, width = whites[0].shape
    return pl.pallas_call(
        product_kernel,
        out_shape=(f32(width, TILE),) * 4 + (f32(depth // 4, width),) * 4,
        in_specs=[VMEM] * 10,
        out_specs=(VMEM,) * 8,
        scratch_shapes=[
            pltpu.VMEM((4, depth, width), jnp.bfloat16),
            pltpu.VMEM((4, depth, width), jnp.bfloat16),
            pltpu.VMEM((depth, width), jnp.float32),
        ],
        compiler_params=PARAMS,
    )(*seps, *whites, *own_white)


def rows_kernel(own, near, across, far, out_ref):
    member = lax.axis_index(("col", "rep"))
    for j, ref in enumerate((own, near, across, far)):
        out_ref[:, pl.ds(pl.multiple_of((member ^ j) * TILE, TILE), TILE)] = ref[...]


def rows_of(pieces):
    count, width = pieces[0].shape
    return pl.pallas_call(
        rows_kernel,
        out_shape=f32(count, 4 * width),
        in_specs=[VMEM] * 4,
        out_specs=VMEM,
        compiler_params=PARAMS,
    )(*pieces)


def diagonal_kernel(own, one, two, three, base_ref, out_ref, variances_ref):
    row, member = lax.axis_index("row"), lax.axis_index(("col", "rep"))
    for j, ref in enumerate((own, one, two, three)):
        columns = pl.ds(pl.multiple_of((row ^ j) * TILE, TILE), TILE)
        out_ref[:, columns] = base_ref[:, columns] + ref[...]
    square = out_ref[:, pl.ds(pl.multiple_of(member * TILE, TILE), TILE)]
    across = lax.broadcasted_iota(jnp.int32, square.shape, 0)
    down = lax.broadcasted_iota(jnp.int32, square.shape, 1)
    variances_ref[...] = jnp.sum(jnp.where(across == down, square, 0.0), axis=0, keepdims=True)


def diagonal(blocks, base):
    return pl.pallas_call(
        diagonal_kernel,
        out_shape=(f32(*base.shape), f32(1, TILE)),
        in_specs=[VMEM] * 5,
        out_specs=(VMEM, VMEM),
        compiler_params=PARAMS,
    )(*blocks, base)


def rows_apart(j):
    return [(i, i ^ j) for i in range(4)]


SWAP = [(0, 1), (1, 0)]


def four_by_four(sep_inverse, row_tiles, panel_rows, diag_inverse):
    quarter = white_quarter(panel_rows, diag_inverse)
    whites = [quarter] + [lax.ppermute(quarter, "row", rows_apart(j)) for j in (1, 2, 3)]

    own = pick(row_tiles, sep_inverse, panel_rows.shape[0] // TILE)
    near = lax.ppermute(own, "rep", SWAP)
    across = lax.ppermute(own, "col", SWAP)
    far = lax.ppermute(across, "rep", SWAP)

    *own_white, base = whiten(panel_rows, diag_inverse)
    out = products((own, near, across, far), whites, own_white)
    terms, pieces = out[:4], out[4:]

    block = terms[0]
    for j in (1, 2, 3):
        block = block + lax.ppermute(terms[j], "row", rows_apart(j))
    blocks = [block] + [lax.ppermute(block, "row", rows_apart(j)) for j in (1, 2, 3)]
    sigma_diag, variances = diagonal(blocks, base)

    sigma_rows = rows_of(
        [
            pieces[0],
            lax.ppermute(pieces[1], "rep", SWAP),
            lax.ppermute(pieces[2], "col", SWAP),
            lax.ppermute(pieces[3], ("col", "rep"), rows_apart(3)),
        ]
    )
    return sigma_rows, sigma_diag, variances.reshape(-1)


def solution(mesh):
    shape = mesh.shape

    def per_device(sep_inverse, row_tiles, panel_rows, diag_inverse):
        square = (shape["row"], shape["col"], shape["rep"]) == (4, 2, 2)
        fits = diag_inverse.shape == (4 * TILE, 4 * TILE) and panel_rows.shape[0] % TILE == 0
        form = four_by_four if square and fits else any_mesh
        return form(sep_inverse, row_tiles, panel_rows, diag_inverse)

    return jax.shard_map(
        per_device,
        mesh=mesh,
        in_specs=(
            P(("groups", "row"), ("col", "rep")),
            P(),
            P(("groups", "row"), None),
            P("groups", None),
        ),
        out_specs=(
            P(("groups", "row", "col", "rep"), None),
            P(("groups", "col", "rep"), None),
            P(("groups", "col", "rep")),
        ),
        check_vma=False,
    )
```

```python
import jax
import jax.numpy as jnp
from jax import lax
from jax.experimental import pallas as pl
from jax.experimental.pallas import tpu as pltpu
from jax.sharding import PartitionSpec as P

TILE = 128
ORDER = (2, 3, 1)
NS = 7
VMEM = pl.BlockSpec(memory_space=pltpu.VMEM)
ANY = pl.BlockSpec(memory_space=pl.ANY)
PARAMS = pltpu.CompilerParams(vmem_limit_bytes=16 * 1024 * 1024)


def broadcast(x, axis, root):
    mine = lax.axis_index(axis) == root
    return lax.psum(jnp.where(mine, x, jnp.zeros_like(x)), axis)


def contract_rows(left, right):
    return lax.dot_general(
        left,
        right,
        (((0,), (0,)), ((), ())),
        precision=lax.Precision.HIGHEST,
        preferred_element_type=jnp.float32,
    )


def any_mesh(sep_inverse, row_tiles, panel_rows, diag_inverse):
    highest = lax.Precision.HIGHEST
    members = lax.axis_size(("col", "rep"))
    column_index = lax.axis_index(("col", "rep"))
    row_index = lax.axis_index("row")
    block_slots = panel_rows.shape[0] // TILE
    block_tiles = sep_inverse.shape[0] // TILE
    width = panel_rows.shape[1]
    own_tiles = (
        lax.dynamic_slice_in_dim(row_tiles, row_index * block_slots, block_slots)
        - row_index * block_tiles
    )
    far_tiles = (
        lax.dynamic_slice_in_dim(row_tiles, column_index * block_slots, block_slots)
        - column_index * block_tiles
    )
    tiled = sep_inverse.reshape(block_tiles, TILE, block_tiles, TILE)
    picked = jnp.take(jnp.take(tiled, own_tiles, axis=0), far_tiles, axis=2)
    picked = picked.reshape(block_slots * TILE, block_slots * TILE)
    own_white = jnp.dot(
        panel_rows, diag_inverse, precision=highest, preferred_element_type=jnp.float32
    )
    far_white = broadcast(own_white, "row", column_index)
    partial_value = -jnp.dot(
        picked, far_white, precision=highest, preferred_element_type=jnp.float32
    )
    piece = partial_value.shape[0] // members
    count = width // members
    first = column_index * count
    sigma_rows = lax.psum_scatter(partial_value, ("col", "rep"), scatter_dimension=0, tiled=True)
    white_mine = lax.dynamic_slice_in_dim(own_white, column_index * piece, piece, 0)
    local_block = lax.psum_scatter(
        contract_rows(sigma_rows, white_mine), ("col", "rep"), scatter_dimension=0, tiled=True
    )
    summed = lax.psum(local_block, "row")
    inverse_cols = lax.dynamic_slice_in_dim(diag_inverse, first, count, 1)
    sigma_diag = contract_rows(inverse_cols, diag_inverse) - summed
    variances = jnp.diagonal(lax.dynamic_slice_in_dim(sigma_diag, first, count, 1))
    return (sigma_rows, sigma_diag, variances)


def split(x):
    high = x.astype(jnp.bfloat16)
    return high, (x - high.astype(jnp.float32)).astype(jnp.bfloat16)


def dot(a, b):
    return jnp.dot(a, b, preferred_element_type=jnp.float32)


def dot3(a, b):
    return dot(a[0], b[0]) + (dot(a[0], b[1]) + dot(a[1], b[0]))


def f32(*shape):
    return jax.ShapeDtypeStruct(shape, jnp.float32)


def first_kernel(
    tiles_hbm, sep_hbm, panel_hbm, inverse_hbm, white_ref, picked_ref, tiles, panel, inverse, sems
):
    row, member = lax.axis_index("row"), lax.axis_index(("col", "rep"))
    columns = pl.ds(pl.multiple_of(member * TILE, TILE), TILE)
    slots, block = picked_ref.shape[0] // TILE, sep_hbm.shape[0] // TILE
    fetch = [
        pltpu.make_async_copy(tiles_hbm, tiles, sems.at[0]),
        pltpu.make_async_copy(panel_hbm, panel, sems.at[1]),
        pltpu.make_async_copy(inverse_hbm.at[:, columns], inverse, sems.at[2]),
    ]
    for copy in fetch:
        copy.start()
    fetch[0].wait()
    picks = []
    for i in range(slots):
        down = (tiles[row * slots + i] - row * block) * TILE
        for j in range(slots):
            across = (tiles[member * slots + j] - member * block) * TILE
            picks.append(
                pltpu.make_async_copy(
                    sep_hbm.at[
                        pl.ds(pl.multiple_of(down, TILE), TILE),
                        pl.ds(pl.multiple_of(across, TILE), TILE),
                    ],
                    picked_ref.at[pl.ds(i * TILE, TILE), pl.ds(j * TILE, TILE)],
                    sems.at[3 + i * slots + j],
                )
            )
    for copy in picks:
        copy.start()
    fetch[1].wait()
    fetch[2].wait()
    white_ref[...] = dot3(split(panel[...]), split(inverse[...]))
    for copy in picks:
        copy.wait()


def first(row_tiles, sep_inverse, panel_rows, diag_inverse):
    slots = panel_rows.shape[0] // TILE
    return pl.pallas_call(
        first_kernel,
        out_shape=(f32(panel_rows.shape[0], TILE), f32(slots * TILE, slots * TILE)),
        in_specs=[ANY] * 4,
        out_specs=(VMEM, VMEM),
        scratch_shapes=[
            pltpu.SMEM(row_tiles.shape, jnp.int32),
            pltpu.VMEM(panel_rows.shape, jnp.float32),
            pltpu.VMEM((diag_inverse.shape[0], TILE), jnp.float32),
            pltpu.SemaphoreType.DMA((3 + slots * slots,)),
        ],
    )(row_tiles, sep_inverse, panel_rows, diag_inverse)


def whiten_kernel(*refs):
    panel_ref, inverse_ref, quarter_ref, own_ref, near_ref = refs[:5]
    high_ref, low_ref, base_ref, quarter_out, own_high, own_low, near_high, near_low = refs[5:]
    member = lax.axis_index(("col", "rep"))
    columns = pl.ds(pl.multiple_of(member * TILE, TILE), TILE)
    inverse = split(inverse_ref[...])
    high_ref[...], low_ref[...] = split(dot3(split(panel_ref[...]), inverse))
    base_ref[...] = dot3(split(inverse_ref[:, columns].T), inverse)
    quarter_out[:, :TILE], quarter_out[:, TILE:] = split(quarter_ref[...])
    own_high[...], own_low[...] = split(own_ref[...])
    near_high[...], near_low[...] = split(near_ref[...])


def whiten(panel_rows, diag_inverse, quarter, own, near):
    def part(*shape):
        return jax.ShapeDtypeStruct(shape, jnp.bfloat16)

    white, sep = part(*panel_rows.shape), part(*own.shape)
    out = pl.pallas_call(
        whiten_kernel,
        out_shape=(
            white,
            white,
            f32(TILE, diag_inverse.shape[1]),
            part(quarter.shape[0], 2 * TILE),
            *[sep] * 4,
        ),
        in_specs=[VMEM] * 5,
        out_specs=(VMEM,) * 8,
        compiler_params=PARAMS,
    )(panel_rows, diag_inverse, quarter, own, near)
    return out[:2], out[2], out[3], out[4:]


def product_kernel(*refs):
    count = len(refs) - 21
    own_high, own_low, near_high, near_low, across, quarter = refs[:6]
    far, whites, (white_high, white_low) = refs[6 : 6 + count], refs[6 + count : 9 + count], refs[9 + count : 11 + count]
    terms, pieces, (joined, product) = refs[-10:-6], refs[-6:-2], refs[-2:]
    row, member = lax.axis_index("row"), lax.axis_index(("col", "rep"))
    joined[row] = quarter[...]
    for j, ref in zip(ORDER, whites):
        joined[row ^ j, :, :TILE], joined[row ^ j, :, TILE:] = split(ref[...])

    def times(high, low, i):
        wide = dot(high, joined[member ^ i])
        return wide[:, :TILE] + (wide[:, TILE:] + dot(low, joined[member ^ i, :, :TILE]))

    total = times(own_high[...], own_low[...], 0) + times(near_high[...], near_low[...], 1)
    total += times(*split(across[...]), 2)
    depth = far[0].shape[0]
    for n, ref in enumerate(far):
        rows = slice(n * depth, (n + 1) * depth)
        product[rows, :] = -(total[rows, :] + times(*split(ref[...]), 3))
    flipped = split(-product[...].T)
    depth = pieces[0].shape[0]
    for j in range(4):
        columns = pl.ds(pl.multiple_of((row ^ j) * TILE, TILE), TILE)
        terms[j][...] = dot3(flipped, (white_high[:, columns], white_low[:, columns]))
        pieces[j][...] = product[pl.ds(pl.multiple_of((member ^ j) * depth, 8), depth), :]


def products(seps, across, quarter, far, whites, own_white):
    depth, width = whites[0].shape
    return pl.pallas_call(
        product_kernel,
        out_shape=(f32(width, TILE),) * 4 + (f32(depth // 4, width),) * 4,
        in_specs=[VMEM] * (11 + len(far)),
        out_specs=(VMEM,) * 8,
        scratch_shapes=[
            pltpu.VMEM((4, depth, 2 * width), jnp.bfloat16),
            pltpu.VMEM((depth, width), jnp.float32),
        ],
        compiler_params=PARAMS,
    )(*seps, across, quarter, *far, *whites, *own_white)


def rows_kernel(own, near, across, far, out_ref):
    member = lax.axis_index(("col", "rep"))
    for j, ref in enumerate((own, near, across, far)):
        out_ref[:, pl.ds(pl.multiple_of((member ^ j) * TILE, TILE), TILE)] = ref[...]


def rows_of(pieces):
    count, width = pieces[0].shape
    return pl.pallas_call(
        rows_kernel,
        out_shape=f32(count, 4 * width),
        in_specs=[VMEM] * 4,
        out_specs=VMEM,
        compiler_params=PARAMS,
    )(*pieces)


def diagonal_kernel(own, first, second, third, base_ref, out_ref, variances_ref):
    row, member = lax.axis_index("row"), lax.axis_index(("col", "rep"))
    for j, ref in zip((0,) + (2, 3, 1), (own, first, second, third)):
        columns = pl.ds(pl.multiple_of((row ^ j) * TILE, TILE), TILE)
        out_ref[:, columns] = base_ref[:, columns] + ref[...]
    square = out_ref[:, pl.ds(pl.multiple_of(member * TILE, TILE), TILE)]
    across = lax.broadcasted_iota(jnp.int32, square.shape, 0)
    down = lax.broadcasted_iota(jnp.int32, square.shape, 1)
    variances_ref[...] = jnp.sum(jnp.where(across == down, square, 0.0), axis=0, keepdims=True)


def diagonal(blocks, base):
    return pl.pallas_call(
        diagonal_kernel,
        out_shape=(f32(*base.shape), f32(1, TILE)),
        in_specs=[VMEM] * 5,
        out_specs=(VMEM, VMEM),
        compiler_params=PARAMS,
    )(*blocks, base)


def rows_apart(j):
    return [(i, i ^ j) for i in range(4)]


SWAP = [(0, 1), (1, 0)]


def four_by_four(sep_inverse, row_tiles, panel_rows, diag_inverse):
    quarter, own = first(row_tiles, sep_inverse, panel_rows, diag_inverse)
    across = lax.ppermute(own, "col", SWAP)
    near = lax.ppermute(own, "rep", SWAP)
    whites = {j: lax.ppermute(quarter, "row", rows_apart(j)) for j in (2, 1)}
    whites[3] = lax.ppermute(whites[2], "row", rows_apart(1))
    own_white, base, split_quarter, seps = whiten(panel_rows, diag_inverse, quarter, own, near)
    across, own_white, base = lax.optimization_barrier((across, own_white, base))
    count = across.shape[0] // 3
    far = [
        lax.ppermute(lax.slice_in_dim(across, i * count, (i + 1) * count), "rep", SWAP)
        for i in range(3)
    ]
    out = products(seps, across, split_quarter, far, [whites[j] for j in ORDER], own_white)
    terms, pieces = out[:4], out[4:]
    got = [lax.ppermute(terms[j], "row", rows_apart(j)) for j in (2, 1, 3)]
    mine = [
        pieces[0],
        lax.ppermute(pieces[1], "rep", SWAP),
        lax.ppermute(pieces[2], "col", SWAP),
        lax.ppermute(pieces[3], ("col", "rep"), rows_apart(3)),
    ]
    got, mine = lax.optimization_barrier((got, mine))
    block = terms[0] + got[0] + got[1] + got[2]
    blocks = [block] + [lax.ppermute(block, "row", rows_apart(j)) for j in (2, 3, 1)]
    sigma_rows = rows_of(mine)
    blocks, sigma_rows = lax.optimization_barrier((blocks, sigma_rows))
    sigma_diag, variances = diagonal(blocks, base)
    return sigma_rows, sigma_diag, variances.reshape(-1)


def solution(mesh):
    shape = mesh.shape

    def per_device(sep_inverse, row_tiles, panel_rows, diag_inverse):
        square = (shape["row"], shape["col"], shape["rep"]) == (4, 2, 2)
        fits = diag_inverse.shape == (4 * TILE, 4 * TILE) and panel_rows.shape[0] % TILE == 0
        form = four_by_four if square and fits else any_mesh
        return form(sep_inverse, row_tiles, panel_rows, diag_inverse)

    return jax.shard_map(
        per_device,
        mesh=mesh,
        in_specs=(
            P(("groups", "row"), ("col", "rep")),
            P(),
            P(("groups", "row"), None),
            P("groups", None),
        ),
        out_specs=(
            P(("groups", "row", "col", "rep"), None),
            P(("groups", "col", "rep"), None),
            P(("groups", "col", "rep")),
        ),
        check_vma=False,
    )
```

```python
import jax
import jax.numpy as jnp
from jax import lax
from jax.experimental import pallas as pl
from jax.experimental.pallas import tpu as pltpu
from jax.sharding import PartitionSpec as P

TILE = 128
ORDER = (2, 3, 1)
NS = 7
VMEM = pl.BlockSpec(memory_space=pltpu.VMEM)
ANY = pl.BlockSpec(memory_space=pl.ANY)
PARAMS = pltpu.CompilerParams(vmem_limit_bytes=16 * 1024 * 1024)


def broadcast(x, axis, root):
    mine = lax.axis_index(axis) == root
    return lax.psum(jnp.where(mine, x, jnp.zeros_like(x)), axis)


def contract_rows(left, right):
    return lax.dot_general(
        left,
        right,
        (((0,), (0,)), ((), ())),
        precision=lax.Precision.HIGHEST,
        preferred_element_type=jnp.float32,
    )


def any_mesh(sep_inverse, row_tiles, panel_rows, diag_inverse):
    highest = lax.Precision.HIGHEST
    members = lax.axis_size(("col", "rep"))
    column_index = lax.axis_index(("col", "rep"))
    row_index = lax.axis_index("row")
    block_slots = panel_rows.shape[0] // TILE
    block_tiles = sep_inverse.shape[0] // TILE
    width = panel_rows.shape[1]
    own_tiles = (
        lax.dynamic_slice_in_dim(row_tiles, row_index * block_slots, block_slots)
        - row_index * block_tiles
    )
    far_tiles = (
        lax.dynamic_slice_in_dim(row_tiles, column_index * block_slots, block_slots)
        - column_index * block_tiles
    )
    tiled = sep_inverse.reshape(block_tiles, TILE, block_tiles, TILE)
    picked = jnp.take(jnp.take(tiled, own_tiles, axis=0), far_tiles, axis=2)
    picked = picked.reshape(block_slots * TILE, block_slots * TILE)
    own_white = jnp.dot(
        panel_rows, diag_inverse, precision=highest, preferred_element_type=jnp.float32
    )
    far_white = broadcast(own_white, "row", column_index)
    partial_value = -jnp.dot(
        picked, far_white, precision=highest, preferred_element_type=jnp.float32
    )
    piece = partial_value.shape[0] // members
    count = width // members
    first = column_index * count
    sigma_rows = lax.psum_scatter(partial_value, ("col", "rep"), scatter_dimension=0, tiled=True)
    white_mine = lax.dynamic_slice_in_dim(own_white, column_index * piece, piece, 0)
    local_block = lax.psum_scatter(
        contract_rows(sigma_rows, white_mine), ("col", "rep"), scatter_dimension=0, tiled=True
    )
    summed = lax.psum(local_block, "row")
    inverse_cols = lax.dynamic_slice_in_dim(diag_inverse, first, count, 1)
    sigma_diag = contract_rows(inverse_cols, diag_inverse) - summed
    variances = jnp.diagonal(lax.dynamic_slice_in_dim(sigma_diag, first, count, 1))
    return (sigma_rows, sigma_diag, variances)


def split(x):
    high = x.astype(jnp.bfloat16)
    return high, (x - high.astype(jnp.float32)).astype(jnp.bfloat16)


def dot(a, b):
    return jnp.dot(a, b, preferred_element_type=jnp.float32)


def dot3(a, b):
    return dot(a[0], b[0]) + (dot(a[0], b[1]) + dot(a[1], b[0]))


def f32(*shape):
    return jax.ShapeDtypeStruct(shape, jnp.float32)


def first_kernel(
    tiles_hbm, sep_hbm, panel_hbm, inverse_hbm, white_ref, picked_ref, tiles, panel, inverse, sems
):
    row, member = lax.axis_index("row"), lax.axis_index(("col", "rep"))
    columns = pl.ds(pl.multiple_of(member * TILE, TILE), TILE)
    slots, block = picked_ref.shape[0] // TILE, sep_hbm.shape[0] // TILE
    fetch = [
        pltpu.make_async_copy(tiles_hbm, tiles, sems.at[0]),
        pltpu.make_async_copy(panel_hbm, panel, sems.at[1]),
        pltpu.make_async_copy(inverse_hbm.at[:, columns], inverse, sems.at[2]),
    ]
    for copy in fetch:
        copy.start()
    fetch[0].wait()
    picks = []
    for i in range(slots):
        down = (tiles[row * slots + i] - row * block) * TILE
        for j in range(slots):
            across = (tiles[member * slots + j] - member * block) * TILE
            picks.append(
                pltpu.make_async_copy(
                    sep_hbm.at[
                        pl.ds(pl.multiple_of(down, TILE), TILE),
                        pl.ds(pl.multiple_of(across, TILE), TILE),
                    ],
                    picked_ref.at[pl.ds(i * TILE, TILE), pl.ds(j * TILE, TILE)],
                    sems.at[3 + i * slots + j],
                )
            )
    for copy in picks:
        copy.start()
    fetch[1].wait()
    fetch[2].wait()
    white_ref[...] = dot3(split(panel[...]), split(inverse[...]))
    for copy in picks:
        copy.wait()


def first(row_tiles, sep_inverse, panel_rows, diag_inverse):
    slots = panel_rows.shape[0] // TILE
    return pl.pallas_call(
        first_kernel,
        out_shape=(f32(panel_rows.shape[0], TILE), f32(slots * TILE, slots * TILE)),
        in_specs=[ANY] * 4,
        out_specs=(VMEM, VMEM),
        scratch_shapes=[
            pltpu.SMEM(row_tiles.shape, jnp.int32),
            pltpu.VMEM(panel_rows.shape, jnp.float32),
            pltpu.VMEM((diag_inverse.shape[0], TILE), jnp.float32),
            pltpu.SemaphoreType.DMA((3 + slots * slots,)),
        ],
    )(row_tiles, sep_inverse, panel_rows, diag_inverse)


def whiten_kernel(*refs):
    panel_ref, inverse_ref, quarter_ref, own_ref, near_ref = refs[:5]
    high_ref, low_ref, base_ref, quarter_out, own_high, own_low, near_high, near_low = refs[5:]
    member = lax.axis_index(("col", "rep"))
    columns = pl.ds(pl.multiple_of(member * TILE, TILE), TILE)
    inverse = split(inverse_ref[...])
    high_ref[...], low_ref[...] = split(dot3(split(panel_ref[...]), inverse))
    base_ref[...] = dot3(split(inverse_ref[:, columns].T), inverse)
    quarter_out[:, :TILE], quarter_out[:, TILE:] = split(quarter_ref[...])
    own_high[...], own_low[...] = split(own_ref[...])
    near_high[...], near_low[...] = split(near_ref[...])


def whiten(panel_rows, diag_inverse, quarter, own, near):
    def part(*shape):
        return jax.ShapeDtypeStruct(shape, jnp.bfloat16)

    white, sep = part(*panel_rows.shape), part(*own.shape)
    out = pl.pallas_call(
        whiten_kernel,
        out_shape=(
            white,
            white,
            f32(TILE, diag_inverse.shape[1]),
            part(quarter.shape[0], 2 * TILE),
            *[sep] * 4,
        ),
        in_specs=[VMEM] * 5,
        out_specs=(VMEM,) * 8,
        compiler_params=PARAMS,
    )(panel_rows, diag_inverse, quarter, own, near)
    return out[:2], out[2], out[3], out[4:]


def product_kernel(*refs):
    count = len(refs) - 19
    own_high, own_low, near_high, near_low, across, quarter = refs[:6]
    far, whites, (white_high, white_low) = refs[6 : 6 + count], refs[6 + count : 9 + count], refs[9 + count : 11 + count]
    terms, pieces, (joined, product) = refs[-8:-4], refs[-4:-2], refs[-2:]
    row, member = lax.axis_index("row"), lax.axis_index(("col", "rep"))
    joined[row] = quarter[...]
    for j, ref in zip(ORDER, whites):
        joined[row ^ j, :, :TILE], joined[row ^ j, :, TILE:] = split(ref[...])

    def times(high, low, i):
        wide = dot(high, joined[member ^ i])
        return wide[:, :TILE] + (wide[:, TILE:] + dot(low, joined[member ^ i, :, :TILE]))

    total = times(own_high[...], own_low[...], 0) + times(near_high[...], near_low[...], 1)
    total += times(*split(across[...]), 2)
    depth = far[0].shape[0]
    for n, ref in enumerate(far):
        rows = slice(n * depth, (n + 1) * depth)
        product[rows, :] = -(total[rows, :] + times(*split(ref[...]), 3))
    flipped = split(-product[...].T)
    depth = pieces[0].shape[0] // 2
    for j in range(4):
        columns = pl.ds(pl.multiple_of((row ^ j) * TILE, TILE), TILE)
        terms[j][...] = dot3(flipped, (white_high[:, columns], white_low[:, columns]))
        mine = pl.ds(pl.multiple_of((member ^ j) * depth, 8), depth)
        pieces[j % 2][j // 2 * depth : (j // 2 + 1) * depth, :] = product[mine, :]


def products(seps, across, quarter, far, whites, own_white):
    depth, width = whites[0].shape
    return pl.pallas_call(
        product_kernel,
        out_shape=(f32(width, TILE),) * 4 + (f32(depth // 2, width),) * 2,
        in_specs=[VMEM] * (11 + len(far)),
        out_specs=(VMEM,) * 6,
        scratch_shapes=[
            pltpu.VMEM((4, depth, 2 * width), jnp.bfloat16),
            pltpu.VMEM((depth, width), jnp.float32),
        ],
        compiler_params=PARAMS,
    )(*seps, across, quarter, *far, *whites, *own_white)


def rows_kernel(own, near, across, far, out_ref):
    member, count = lax.axis_index(("col", "rep")), out_ref.shape[0]
    blocks = (own[:count, :], near[:count, :], across[...], far[...])
    for j, block in enumerate(blocks):
        out_ref[:, pl.ds(pl.multiple_of((member ^ j) * TILE, TILE), TILE)] = block


def rows_of(own, near, across, far):
    count, width = own.shape
    return pl.pallas_call(
        rows_kernel,
        out_shape=f32(count // 2, 4 * width),
        in_specs=[VMEM] * 4,
        out_specs=VMEM,
        compiler_params=PARAMS,
    )(own, near, across, far)


def diagonal_kernel(own, first, second, third, base_ref, out_ref, variances_ref):
    row, member = lax.axis_index("row"), lax.axis_index(("col", "rep"))
    for j, ref in zip((0,) + (2, 3, 1), (own, first, second, third)):
        columns = pl.ds(pl.multiple_of((row ^ j) * TILE, TILE), TILE)
        out_ref[:, columns] = base_ref[:, columns] + ref[...]
    square = out_ref[:, pl.ds(pl.multiple_of(member * TILE, TILE), TILE)]
    across = lax.broadcasted_iota(jnp.int32, square.shape, 0)
    down = lax.broadcasted_iota(jnp.int32, square.shape, 1)
    variances_ref[...] = jnp.sum(jnp.where(across == down, square, 0.0), axis=0, keepdims=True)


def diagonal(blocks, base):
    return pl.pallas_call(
        diagonal_kernel,
        out_shape=(f32(*base.shape), f32(1, TILE)),
        in_specs=[VMEM] * 5,
        out_specs=(VMEM, VMEM),
        compiler_params=PARAMS,
    )(*blocks, base)


def rows_apart(j):
    return [(i, i ^ j) for i in range(4)]


SWAP = [(0, 1), (1, 0)]


def four_by_four(sep_inverse, row_tiles, panel_rows, diag_inverse):
    quarter, own = first(row_tiles, sep_inverse, panel_rows, diag_inverse)
    across = lax.ppermute(own, "col", SWAP)
    near = lax.ppermute(own, "rep", SWAP)
    whites = {j: lax.ppermute(quarter, "row", rows_apart(j)) for j in (2, 1)}
    whites[3] = lax.ppermute(whites[2], "row", rows_apart(1))
    own_white, base, split_quarter, seps = whiten(panel_rows, diag_inverse, quarter, own, near)
    across, own_white, base = lax.optimization_barrier((across, own_white, base))
    count = across.shape[0] // 3
    far = [
        lax.ppermute(lax.slice_in_dim(across, i * count, (i + 1) * count), "rep", SWAP)
        for i in range(3)
    ]
    out = products(seps, across, split_quarter, far, [whites[j] for j in ORDER], own_white)
    terms, (mine, others) = out[:4], out[4:]
    near = lax.ppermute(others, "rep", SWAP)
    got = [lax.ppermute(terms[j], "row", rows_apart(j)) for j in (2, 1, 3)]
    count = mine.shape[0] // 2
    across = lax.ppermute(mine[count:], "col", SWAP)
    far = lax.ppermute(near[count:], "col", SWAP)
    block = terms[0] + got[0] + got[1] + got[2]
    again, across, far = lax.optimization_barrier((block, across, far))
    blocks = [block] + [lax.ppermute(block, "row", rows_apart(j)) for j in (2, 3)] + [lax.ppermute(again, "row", rows_apart(1))]
    sigma_rows = rows_of(mine, near, across, far)
    blocks, sigma_rows = lax.optimization_barrier((blocks, sigma_rows))
    sigma_diag, variances = diagonal(blocks, base)
    return sigma_rows, sigma_diag, variances.reshape(-1)


def solution(mesh):
    shape = mesh.shape

    def per_device(sep_inverse, row_tiles, panel_rows, diag_inverse):
        square = (shape["row"], shape["col"], shape["rep"]) == (4, 2, 2)
        fits = diag_inverse.shape == (4 * TILE, 4 * TILE) and panel_rows.shape[0] % TILE == 0
        form = four_by_four if square and fits else any_mesh
        return form(sep_inverse, row_tiles, panel_rows, diag_inverse)

    return jax.shard_map(
        per_device,
        mesh=mesh,
        in_specs=(
            P(("groups", "row"), ("col", "rep")),
            P(),
            P(("groups", "row"), None),
            P("groups", None),
        ),
        out_specs=(
            P(("groups", "row", "col", "rep"), None),
            P(("groups", "col", "rep"), None),
            P(("groups", "col", "rep")),
        ),
        check_vma=False,
    )
```

```python
import jax
import jax.numpy as jnp
from jax import lax
from jax.experimental import pallas as pl
from jax.experimental.pallas import tpu as pltpu
from jax.sharding import PartitionSpec as P

TILE = 128
ORDER = (2, 3, 1)
NS = 7
VMEM = pl.BlockSpec(memory_space=pltpu.VMEM)
ANY = pl.BlockSpec(memory_space=pl.ANY)
PARAMS = pltpu.CompilerParams(vmem_limit_bytes=16 * 1024 * 1024)


def broadcast(x, axis, root):
    mine = lax.axis_index(axis) == root
    return lax.psum(jnp.where(mine, x, jnp.zeros_like(x)), axis)


def contract_rows(left, right):
    return lax.dot_general(
        left,
        right,
        (((0,), (0,)), ((), ())),
        precision=lax.Precision.HIGHEST,
        preferred_element_type=jnp.float32,
    )


def any_mesh(sep_inverse, row_tiles, panel_rows, diag_inverse):
    highest = lax.Precision.HIGHEST
    members = lax.axis_size(("col", "rep"))
    column_index = lax.axis_index(("col", "rep"))
    row_index = lax.axis_index("row")
    block_slots = panel_rows.shape[0] // TILE
    block_tiles = sep_inverse.shape[0] // TILE
    width = panel_rows.shape[1]
    own_tiles = (
        lax.dynamic_slice_in_dim(row_tiles, row_index * block_slots, block_slots)
        - row_index * block_tiles
    )
    far_tiles = (
        lax.dynamic_slice_in_dim(row_tiles, column_index * block_slots, block_slots)
        - column_index * block_tiles
    )
    tiled = sep_inverse.reshape(block_tiles, TILE, block_tiles, TILE)
    picked = jnp.take(jnp.take(tiled, own_tiles, axis=0), far_tiles, axis=2)
    picked = picked.reshape(block_slots * TILE, block_slots * TILE)
    own_white = jnp.dot(
        panel_rows, diag_inverse, precision=highest, preferred_element_type=jnp.float32
    )
    far_white = broadcast(own_white, "row", column_index)
    partial_value = -jnp.dot(
        picked, far_white, precision=highest, preferred_element_type=jnp.float32
    )
    piece = partial_value.shape[0] // members
    count = width // members
    first = column_index * count
    sigma_rows = lax.psum_scatter(partial_value, ("col", "rep"), scatter_dimension=0, tiled=True)
    white_mine = lax.dynamic_slice_in_dim(own_white, column_index * piece, piece, 0)
    local_block = lax.psum_scatter(
        contract_rows(sigma_rows, white_mine), ("col", "rep"), scatter_dimension=0, tiled=True
    )
    summed = lax.psum(local_block, "row")
    inverse_cols = lax.dynamic_slice_in_dim(diag_inverse, first, count, 1)
    sigma_diag = contract_rows(inverse_cols, diag_inverse) - summed
    variances = jnp.diagonal(lax.dynamic_slice_in_dim(sigma_diag, first, count, 1))
    return (sigma_rows, sigma_diag, variances)


def split(x):
    high = x.astype(jnp.bfloat16)
    return high, (x - high.astype(jnp.float32)).astype(jnp.bfloat16)


def dot(a, b):
    return jnp.dot(a, b, preferred_element_type=jnp.float32)


def dot3(a, b):
    return dot(a[0], b[0]) + (dot(a[0], b[1]) + dot(a[1], b[0]))


def f32(*shape):
    return jax.ShapeDtypeStruct(shape, jnp.float32)


def first_kernel(
    tiles_hbm, sep_hbm, panel_hbm, inverse_hbm, white_ref, picked_ref, tiles, panel, inverse, sems
):
    row, member = lax.axis_index("row"), lax.axis_index(("col", "rep"))
    columns = pl.ds(pl.multiple_of(member * TILE, TILE), TILE)
    slots, block = picked_ref.shape[0] // TILE, sep_hbm.shape[0] // TILE
    fetch = [
        pltpu.make_async_copy(tiles_hbm, tiles, sems.at[0]),
        pltpu.make_async_copy(panel_hbm, panel, sems.at[1]),
        pltpu.make_async_copy(inverse_hbm.at[:, columns], inverse, sems.at[2]),
    ]
    for copy in fetch:
        copy.start()
    fetch[0].wait()
    picks = []
    for i in range(slots):
        down = (tiles[row * slots + i] - row * block) * TILE
        for j in range(slots):
            across = (tiles[member * slots + j] - member * block) * TILE
            picks.append(
                pltpu.make_async_copy(
                    sep_hbm.at[
                        pl.ds(pl.multiple_of(down, TILE), TILE),
                        pl.ds(pl.multiple_of(across, TILE), TILE),
                    ],
                    picked_ref.at[pl.ds(i * TILE, TILE), pl.ds(j * TILE, TILE)],
                    sems.at[3 + i * slots + j],
                )
            )
    for copy in picks:
        copy.start()
    fetch[1].wait()
    fetch[2].wait()
    white_ref[...] = dot3(split(panel[...]), split(inverse[...]))
    for copy in picks:
        copy.wait()


def first(row_tiles, sep_inverse, panel_rows, diag_inverse):
    slots = panel_rows.shape[0] // TILE
    return pl.pallas_call(
        first_kernel,
        out_shape=(f32(panel_rows.shape[0], TILE), f32(slots * TILE, slots * TILE)),
        in_specs=[ANY] * 4,
        out_specs=(VMEM, VMEM),
        scratch_shapes=[
            pltpu.SMEM(row_tiles.shape, jnp.int32),
            pltpu.VMEM(panel_rows.shape, jnp.float32),
            pltpu.VMEM((diag_inverse.shape[0], TILE), jnp.float32),
            pltpu.SemaphoreType.DMA((3 + slots * slots,)),
        ],
    )(row_tiles, sep_inverse, panel_rows, diag_inverse)


def whiten_kernel(*refs):
    panel_ref, inverse_ref, quarter_ref, own_ref, near_ref = refs[:5]
    high_ref, low_ref, base_ref, quarter_out, sep_high, sep_low = refs[5:]
    member = lax.axis_index(("col", "rep"))
    columns = pl.ds(pl.multiple_of(member * TILE, TILE), TILE)
    inverse = split(inverse_ref[...])
    high_ref[...], low_ref[...] = split(dot3(split(panel_ref[...]), inverse))
    base_ref[...] = dot3(split(inverse_ref[:, columns].T), inverse)
    quarter_out[:, :TILE], quarter_out[:, TILE:] = split(quarter_ref[...])
    depth = own_ref.shape[1]
    sep_high[:, :depth], sep_low[:, :depth] = split(own_ref[...])
    sep_high[:, depth:], sep_low[:, depth:] = split(near_ref[...])


def whiten(panel_rows, diag_inverse, quarter, own, near):
    def part(*shape):
        return jax.ShapeDtypeStruct(shape, jnp.bfloat16)

    white, sep = part(*panel_rows.shape), part(own.shape[0], 2 * own.shape[1])
    out = pl.pallas_call(
        whiten_kernel,
        out_shape=(
            white,
            white,
            f32(TILE, diag_inverse.shape[1]),
            part(quarter.shape[0], 2 * TILE),
            *[sep] * 2,
        ),
        in_specs=[VMEM] * 5,
        out_specs=(VMEM,) * 6,
        compiler_params=PARAMS,
    )(panel_rows, diag_inverse, quarter, own, near)
    return out[:2], out[2], out[3], out[4:]


def product_kernel(*refs):
    sep_high, sep_low, across, quarter, *far = refs[:-15]
    whites, (white_high, white_low) = refs[-15:-12], refs[-12:-10]
    terms, pieces, (joined, product, other_high, other_low) = refs[-10:-6], refs[-6:-4], refs[-4:]
    row, member = lax.axis_index("row"), lax.axis_index(("col", "rep"))
    depth = across.shape[1]

    def place(j):
        return pl.ds(pl.multiple_of((row ^ j ^ member) * depth, TILE), depth)

    joined[place(0), :] = quarter[...]
    for j, ref in zip(ORDER, whites):
        joined[place(j), :TILE], joined[place(j), TILE:] = split(ref[...])
    other_high[:, :depth], other_low[:, :depth] = split(across[...])
    count = far[0].shape[0]
    for n, ref in enumerate(far):
        rows = slice(n * count, (n + 1) * count)
        other_high[rows, depth:], other_low[rows, depth:] = split(ref[...])
    wide = dot(sep_high[...], joined[: 2 * depth, :]) + dot(other_high[...], joined[2 * depth :, :])
    low = dot(sep_low[...], joined[: 2 * depth, :TILE]) + dot(other_low[...], joined[2 * depth :, :TILE])
    total = wide[:, :TILE] + (wide[:, TILE:] + low)
    product[...] = -total
    flipped = split(total.T)
    stacked = jnp.concatenate(flipped)
    depth = pieces[0].shape[0] // 2
    both = dot(stacked, white_high[...])
    full = both[:TILE] + (both[TILE:] + dot(flipped[0], white_low[...]))
    for j in range(4):
        value = full[:, :TILE]
        for n in range(1, 4):
            value = jnp.where((row ^ j) == n, full[:, n * TILE : (n + 1) * TILE], value)
        terms[j][...] = value
        mine = pl.ds(pl.multiple_of((member ^ j) * depth, 8), depth)
        pieces[j % 2][j // 2 * depth : (j // 2 + 1) * depth, :] = product[mine, :]


def products(seps, across, quarter, far, whites, own_white):
    depth, width = whites[0].shape
    return pl.pallas_call(
        product_kernel,
        out_shape=(f32(width, TILE),) * 4 + (f32(depth // 2, width),) * 2,
        in_specs=[VMEM] * (9 + len(far)),
        out_specs=(VMEM,) * 6,
        scratch_shapes=[
            pltpu.VMEM((4 * depth, 2 * width), jnp.bfloat16),
            pltpu.VMEM((depth, width), jnp.float32),
            pltpu.VMEM((depth, 2 * depth), jnp.bfloat16),
            pltpu.VMEM((depth, 2 * depth), jnp.bfloat16),
        ],
        compiler_params=PARAMS,
    )(*seps, across, quarter, *far, *whites, *own_white)


def rows_kernel(own, near, across, far, out_ref):
    member, count = lax.axis_index(("col", "rep")), out_ref.shape[0]
    blocks = (own[:count, :], near[:count, :], across[...], far[...])
    for j, block in enumerate(blocks):
        out_ref[:, pl.ds(pl.multiple_of((member ^ j) * TILE, TILE), TILE)] = block


def rows_of(own, near, across, far):
    count, width = own.shape
    return pl.pallas_call(
        rows_kernel,
        out_shape=f32(count // 2, 4 * width),
        in_specs=[VMEM] * 4,
        out_specs=VMEM,
        compiler_params=PARAMS,
    )(own, near, across, far)


def diagonal_kernel(own, first, second, third, base_ref, out_ref, variances_ref):
    row, member = lax.axis_index("row"), lax.axis_index(("col", "rep"))
    for j, ref in zip((0,) + (2, 3, 1), (own, first, second, third)):
        columns = pl.ds(pl.multiple_of((row ^ j) * TILE, TILE), TILE)
        out_ref[:, columns] = base_ref[:, columns] + ref[...]
    square = out_ref[:, pl.ds(pl.multiple_of(member * TILE, TILE), TILE)]
    across = lax.broadcasted_iota(jnp.int32, square.shape, 0)
    down = lax.broadcasted_iota(jnp.int32, square.shape, 1)
    variances_ref[...] = jnp.sum(jnp.where(across == down, square, 0.0), axis=0, keepdims=True)


def diagonal(blocks, base):
    return pl.pallas_call(
        diagonal_kernel,
        out_shape=(f32(*base.shape), f32(1, TILE)),
        in_specs=[VMEM] * 5,
        out_specs=(VMEM, VMEM),
        compiler_params=PARAMS,
    )(*blocks, base)


def rows_apart(j):
    return [(i, i ^ j) for i in range(4)]


SWAP = [(0, 1), (1, 0)]


def four_by_four(sep_inverse, row_tiles, panel_rows, diag_inverse):
    quarter, own = first(row_tiles, sep_inverse, panel_rows, diag_inverse)
    across = lax.ppermute(own, "col", SWAP)
    near = lax.ppermute(own, "rep", SWAP)
    whites = {j: lax.ppermute(quarter, "row", rows_apart(j)) for j in (3, 1)}
    whites[2] = lax.ppermute(whites[3], "row", rows_apart(1))
    own_white, base, split_quarter, seps = whiten(panel_rows, diag_inverse, quarter, own, near)
    across, own_white, base = lax.optimization_barrier((across, own_white, base))
    count = across.shape[0] // 3
    far = [
        lax.ppermute(lax.slice_in_dim(across, i * count, (i + 1) * count), "rep", SWAP)
        for i in range(3)
    ]
    out = products(seps, across, split_quarter, far, [whites[j] for j in ORDER], own_white)
    terms, (mine, others) = out[:4], out[4:]
    near = lax.ppermute(others, "rep", SWAP)
    got = [lax.ppermute(terms[j], "row", rows_apart(j)) for j in (2, 1, 3)]
    count = mine.shape[0] // 2
    across = lax.ppermute(mine[count:], "col", SWAP)
    far = lax.ppermute(near[count:], "col", SWAP)
    block = terms[0] + got[0] + got[1] + got[2]
    again, across, far = lax.optimization_barrier((block, across, far))
    blocks = [block] + [lax.ppermute(block, "row", rows_apart(j)) for j in (2, 3)] + [lax.ppermute(again, "row", rows_apart(1))]
    sigma_rows = rows_of(mine, near, across, far)
    blocks, sigma_rows = lax.optimization_barrier((blocks, sigma_rows))
    sigma_diag, variances = diagonal(blocks, base)
    return sigma_rows, sigma_diag, variances.reshape(-1)


def solution(mesh):
    shape = mesh.shape

    def per_device(sep_inverse, row_tiles, panel_rows, diag_inverse):
        square = (shape["row"], shape["col"], shape["rep"]) == (4, 2, 2)
        fits = diag_inverse.shape == (4 * TILE, 4 * TILE) and panel_rows.shape[0] % TILE == 0
        form = four_by_four if square and fits else any_mesh
        return form(sep_inverse, row_tiles, panel_rows, diag_inverse)

    return jax.shard_map(
        per_device,
        mesh=mesh,
        in_specs=(
            P(("groups", "row"), ("col", "rep")),
            P(),
            P(("groups", "row"), None),
            P("groups", None),
        ),
        out_specs=(
            P(("groups", "row", "col", "rep"), None),
            P(("groups", "col", "rep"), None),
            P(("groups", "col", "rep")),
        ),
        check_vma=False,
    )
```

```python
import jax
import jax.numpy as jnp
from jax import lax
from jax.experimental import pallas as pl
from jax.experimental.pallas import tpu as pltpu
from jax.sharding import PartitionSpec as P

TILE = 128
ORDER = (2, 3, 1)
VMEM = pl.BlockSpec(memory_space=pltpu.VMEM)
ANY = pl.BlockSpec(memory_space=pl.ANY)
PARAMS = pltpu.CompilerParams(vmem_limit_bytes=16 * 1024 * 1024)


def broadcast(x, axis, root):
    mine = lax.axis_index(axis) == root
    return lax.psum(jnp.where(mine, x, jnp.zeros_like(x)), axis)


def contract_rows(left, right):
    return lax.dot_general(
        left,
        right,
        (((0,), (0,)), ((), ())),
        precision=lax.Precision.HIGHEST,
        preferred_element_type=jnp.float32,
    )


def any_mesh(sep_inverse, row_tiles, panel_rows, diag_inverse):
    highest = lax.Precision.HIGHEST
    members = lax.axis_size(("col", "rep"))
    column_index = lax.axis_index(("col", "rep"))
    row_index = lax.axis_index("row")
    block_slots = panel_rows.shape[0] // TILE
    block_tiles = sep_inverse.shape[0] // TILE
    width = panel_rows.shape[1]
    own_tiles = (
        lax.dynamic_slice_in_dim(row_tiles, row_index * block_slots, block_slots)
        - row_index * block_tiles
    )
    far_tiles = (
        lax.dynamic_slice_in_dim(row_tiles, column_index * block_slots, block_slots)
        - column_index * block_tiles
    )
    tiled = sep_inverse.reshape(block_tiles, TILE, block_tiles, TILE)
    picked = jnp.take(jnp.take(tiled, own_tiles, axis=0), far_tiles, axis=2)
    picked = picked.reshape(block_slots * TILE, block_slots * TILE)
    own_white = jnp.dot(
        panel_rows, diag_inverse, precision=highest, preferred_element_type=jnp.float32
    )
    far_white = broadcast(own_white, "row", column_index)
    partial_value = -jnp.dot(
        picked, far_white, precision=highest, preferred_element_type=jnp.float32
    )
    piece = partial_value.shape[0] // members
    count = width // members
    first = column_index * count
    sigma_rows = lax.psum_scatter(partial_value, ("col", "rep"), scatter_dimension=0, tiled=True)
    white_mine = lax.dynamic_slice_in_dim(own_white, column_index * piece, piece, 0)
    local_block = lax.psum_scatter(
        contract_rows(sigma_rows, white_mine), ("col", "rep"), scatter_dimension=0, tiled=True
    )
    summed = lax.psum(local_block, "row")
    inverse_cols = lax.dynamic_slice_in_dim(diag_inverse, first, count, 1)
    sigma_diag = contract_rows(inverse_cols, diag_inverse) - summed
    variances = jnp.diagonal(lax.dynamic_slice_in_dim(sigma_diag, first, count, 1))
    return (sigma_rows, sigma_diag, variances)


def split(x):
    high = x.astype(jnp.bfloat16)
    return high, (x - high.astype(jnp.float32)).astype(jnp.bfloat16)


def dot(a, b):
    return jnp.dot(a, b, preferred_element_type=jnp.float32)


def dot3(a, b):
    return dot(a[0], b[0]) + (dot(a[0], b[1]) + dot(a[1], b[0]))


def f32(*shape):
    return jax.ShapeDtypeStruct(shape, jnp.float32)


def first_kernel(
    tiles_hbm, sep_hbm, panel_hbm, inverse_hbm, white_ref, picked_ref, tiles, panel, inverse, sems
):
    row, member = lax.axis_index("row"), lax.axis_index(("col", "rep"))
    columns = pl.ds(pl.multiple_of(member * TILE, TILE), TILE)
    slots, block = picked_ref.shape[0] // TILE, sep_hbm.shape[0] // TILE
    fetch = [
        pltpu.make_async_copy(tiles_hbm, tiles, sems.at[0]),
        pltpu.make_async_copy(panel_hbm, panel, sems.at[1]),
        pltpu.make_async_copy(inverse_hbm.at[:, columns], inverse, sems.at[2]),
    ]
    for copy in fetch:
        copy.start()
    fetch[0].wait()
    picks = []
    for i in range(slots):
        down = (tiles[row * slots + i] - row * block) * TILE
        for j in range(slots):
            across = (tiles[member * slots + j] - member * block) * TILE
            picks.append(
                pltpu.make_async_copy(
                    sep_hbm.at[
                        pl.ds(pl.multiple_of(down, TILE), TILE),
                        pl.ds(pl.multiple_of(across, TILE), TILE),
                    ],
                    picked_ref.at[pl.ds(i * TILE, TILE), pl.ds(j * TILE, TILE)],
                    sems.at[3 + i * slots + j],
                )
            )
    for copy in picks:
        copy.start()
    fetch[1].wait()
    fetch[2].wait()
    high, low = split(panel[...])
    parts = split(inverse[...])
    wide = dot(high, jnp.concatenate(parts, axis=1))
    white_ref[...] = wide[:, :TILE] + (wide[:, TILE:] + dot(low, parts[0]))
    for copy in picks:
        copy.wait()


def first(row_tiles, sep_inverse, panel_rows, diag_inverse):
    slots = panel_rows.shape[0] // TILE
    return pl.pallas_call(
        first_kernel,
        out_shape=(f32(panel_rows.shape[0], TILE), f32(slots * TILE, slots * TILE)),
        in_specs=[ANY] * 4,
        out_specs=(VMEM, VMEM),
        scratch_shapes=[
            pltpu.SMEM(row_tiles.shape, jnp.int32),
            pltpu.VMEM(panel_rows.shape, jnp.float32),
            pltpu.VMEM((diag_inverse.shape[0], TILE), jnp.float32),
            pltpu.SemaphoreType.DMA((3 + slots * slots,)),
        ],
    )(row_tiles, sep_inverse, panel_rows, diag_inverse)


def whiten_kernel(*refs):
    panel_ref, inverse_ref, quarter_ref, own_ref, near_ref = refs[:5]
    high_ref, low_ref, base_ref, quarter_out, sep_high, sep_low = refs[5:]
    member = lax.axis_index(("col", "rep"))
    columns = pl.ds(pl.multiple_of(member * TILE, TILE), TILE)
    inverse = split(inverse_ref[...])
    high_ref[...], low_ref[...] = split(dot3(split(panel_ref[...]), inverse))
    base_ref[...] = dot3(split(inverse_ref[:, columns].T), inverse)
    quarter_out[:, :TILE], quarter_out[:, TILE:] = split(quarter_ref[...])
    depth = own_ref.shape[1]
    sep_high[:, :depth], sep_low[:, :depth] = split(own_ref[...])
    sep_high[:, depth:], sep_low[:, depth:] = split(near_ref[...])


def whiten(panel_rows, diag_inverse, quarter, own, near):
    def part(*shape):
        return jax.ShapeDtypeStruct(shape, jnp.bfloat16)

    white, sep = part(*panel_rows.shape), part(own.shape[0], 2 * own.shape[1])
    out = pl.pallas_call(
        whiten_kernel,
        out_shape=(
            white,
            white,
            f32(TILE, diag_inverse.shape[1]),
            part(quarter.shape[0], 2 * TILE),
            *[sep] * 2,
        ),
        in_specs=[VMEM] * 5,
        out_specs=(VMEM,) * 6,
        compiler_params=PARAMS,
    )(panel_rows, diag_inverse, quarter, own, near)
    return out[:2], out[2], out[3], out[4:]


def product_kernel(*refs):
    sep_high, sep_low, across, quarter, *far = refs[:-15]
    whites, (white_high, white_low) = refs[-15:-12], refs[-12:-10]
    terms, pieces, (joined, product, other_high, other_low) = refs[-10:-6], refs[-6:-4], refs[-4:]
    row, member = lax.axis_index("row"), lax.axis_index(("col", "rep"))
    depth = across.shape[1]

    def place(j):
        return pl.ds(pl.multiple_of((row ^ j ^ member) * depth, TILE), depth)

    joined[place(0), :] = quarter[...]
    for j, ref in zip(ORDER, whites):
        joined[place(j), :TILE], joined[place(j), TILE:] = split(ref[...])
    other_high[:, :depth], other_low[:, :depth] = split(across[...])
    count = far[0].shape[0]
    for n, ref in enumerate(far):
        rows = slice(n * count, (n + 1) * count)
        other_high[rows, depth:], other_low[rows, depth:] = split(ref[...])
    wide = dot(sep_high[...], joined[: 2 * depth, :]) + dot(other_high[...], joined[2 * depth :, :])
    low = dot(sep_low[...], joined[: 2 * depth, :TILE]) + dot(other_low[...], joined[2 * depth :, :TILE])
    total = wide[:, :TILE] + (wide[:, TILE:] + low)
    product[...] = -total
    flipped = split(total.T)
    stacked = jnp.concatenate(flipped)
    depth = pieces[0].shape[0] // 2
    both = dot(stacked, white_high[...])
    full = both[:TILE] + (both[TILE:] + dot(flipped[0], white_low[...]))
    for j in range(4):
        value = full[:, :TILE]
        for n in range(1, 4):
            value = jnp.where((row ^ j) == n, full[:, n * TILE : (n + 1) * TILE], value)
        terms[j][...] = value
        mine = pl.ds(pl.multiple_of((member ^ j) * depth, 8), depth)
        pieces[j % 2][j // 2 * depth : (j // 2 + 1) * depth, :] = product[mine, :]


def products(seps, across, quarter, far, whites, own_white):
    depth, width = whites[0].shape
    return pl.pallas_call(
        product_kernel,
        out_shape=(f32(width, TILE),) * 4 + (f32(depth // 2, width),) * 2,
        in_specs=[VMEM] * (9 + len(far)),
        out_specs=(VMEM,) * 6,
        scratch_shapes=[
            pltpu.VMEM((4 * depth, 2 * width), jnp.bfloat16),
            pltpu.VMEM((depth, width), jnp.float32),
            pltpu.VMEM((depth, 2 * depth), jnp.bfloat16),
            pltpu.VMEM((depth, 2 * depth), jnp.bfloat16),
        ],
        compiler_params=PARAMS,
    )(*seps, across, quarter, *far, *whites, *own_white)


def rows_kernel(own, near, across, far, out_ref):
    member, count = lax.axis_index(("col", "rep")), out_ref.shape[0]
    blocks = (own[:count, :], near[:count, :], across[...], far[...])
    for j, block in enumerate(blocks):
        out_ref[:, pl.ds(pl.multiple_of((member ^ j) * TILE, TILE), TILE)] = block


def rows_of(own, near, across, far):
    count, width = own.shape
    return pl.pallas_call(
        rows_kernel,
        out_shape=f32(count // 2, 4 * width),
        in_specs=[VMEM] * 4,
        out_specs=VMEM,
        compiler_params=PARAMS,
    )(own, near, across, far)


def diagonal_kernel(own, first, second, third, base_ref, out_ref, variances_ref):
    row, member = lax.axis_index("row"), lax.axis_index(("col", "rep"))
    for j, ref in zip((0,) + ORDER, (own, first, second, third)):
        columns = pl.ds(pl.multiple_of((row ^ j) * TILE, TILE), TILE)
        out_ref[:, columns] = base_ref[:, columns] + ref[...]
    square = out_ref[:, pl.ds(pl.multiple_of(member * TILE, TILE), TILE)]
    across = lax.broadcasted_iota(jnp.int32, square.shape, 0)
    down = lax.broadcasted_iota(jnp.int32, square.shape, 1)
    variances_ref[...] = jnp.sum(jnp.where(across == down, square, 0.0), axis=0, keepdims=True)


def diagonal(blocks, base):
    return pl.pallas_call(
        diagonal_kernel,
        out_shape=(f32(*base.shape), f32(1, TILE)),
        in_specs=[VMEM] * 5,
        out_specs=(VMEM, VMEM),
        compiler_params=PARAMS,
    )(*blocks, base)


def rows_apart(j):
    return [(i, i ^ j) for i in range(4)]


SWAP = [(0, 1), (1, 0)]


def four_by_four(sep_inverse, row_tiles, panel_rows, diag_inverse):
    quarter, own = first(row_tiles, sep_inverse, panel_rows, diag_inverse)
    across = lax.ppermute(own, "col", SWAP)
    near = lax.ppermute(own, "rep", SWAP)
    whites = {j: lax.ppermute(quarter, "row", rows_apart(j)) for j in (3, 1)}
    whites[2] = lax.ppermute(whites[3], "row", rows_apart(1))
    own_white, base, split_quarter, seps = whiten(panel_rows, diag_inverse, quarter, own, near)
    across, own_white, base = lax.optimization_barrier((across, own_white, base))
    count = across.shape[0] // 3
    far = [
        lax.ppermute(lax.slice_in_dim(across, i * count, (i + 1) * count), "rep", SWAP)
        for i in range(3)
    ]
    out = products(seps, across, split_quarter, far, [whites[j] for j in ORDER], own_white)
    terms, (mine, others) = out[:4], out[4:]
    near = lax.ppermute(others, "rep", SWAP)
    got = [lax.ppermute(terms[j], "row", rows_apart(j)) for j in (2, 1, 3)]
    count = mine.shape[0] // 2
    across = lax.ppermute(mine[count:], "col", SWAP)
    far = lax.ppermute(near[count:], "col", SWAP)
    block = terms[0] + got[0] + got[1] + got[2]
    again, across, far = lax.optimization_barrier((block, across, far))
    sent = zip(ORDER, (block, block, again))
    blocks = [block] + [lax.ppermute(x, "row", rows_apart(j)) for j, x in sent]
    sigma_rows = rows_of(mine, near, across, far)
    blocks, sigma_rows = lax.optimization_barrier((blocks, sigma_rows))
    sigma_diag, variances = diagonal(blocks, base)
    return sigma_rows, sigma_diag, variances.reshape(-1)


def solution(mesh):
    shape = mesh.shape

    def per_device(sep_inverse, row_tiles, panel_rows, diag_inverse):
        square = (shape["row"], shape["col"], shape["rep"]) == (4, 2, 2)
        fits = diag_inverse.shape == (4 * TILE, 4 * TILE) and panel_rows.shape[0] % (3 * TILE) == 0
        form = four_by_four if square and fits else any_mesh
        return form(sep_inverse, row_tiles, panel_rows, diag_inverse)

    return jax.shard_map(
        per_device,
        mesh=mesh,
        in_specs=(
            P(("groups", "row"), ("col", "rep")),
            P(),
            P(("groups", "row"), None),
            P("groups", None),
        ),
        out_specs=(
            P(("groups", "row", "col", "rep"), None),
            P(("groups", "col", "rep"), None),
            P(("groups", "col", "rep")),
        ),
        check_vma=False,
    )
```

```python
import jax
import jax.numpy as jnp
from jax import lax
from jax.experimental import pallas as pl
from jax.experimental.pallas import tpu as pltpu
from jax.sharding import PartitionSpec as P

TILE = 128
ORDER = (2, 3, 1)
VMEM = pl.BlockSpec(memory_space=pltpu.VMEM)
ANY = pl.BlockSpec(memory_space=pl.ANY)
PARAMS = pltpu.CompilerParams(vmem_limit_bytes=16 * 1024 * 1024)


def broadcast(x, axis, root):
    mine = lax.axis_index(axis) == root
    return lax.psum(jnp.where(mine, x, jnp.zeros_like(x)), axis)


def contract_rows(left, right):
    return lax.dot_general(
        left,
        right,
        (((0,), (0,)), ((), ())),
        precision=lax.Precision.HIGHEST,
        preferred_element_type=jnp.float32,
    )


def any_mesh(sep_inverse, row_tiles, panel_rows, diag_inverse):
    highest = lax.Precision.HIGHEST
    members = lax.axis_size(("col", "rep"))
    column_index = lax.axis_index(("col", "rep"))
    row_index = lax.axis_index("row")
    block_slots = panel_rows.shape[0] // TILE
    block_tiles = sep_inverse.shape[0] // TILE
    width = panel_rows.shape[1]
    own_tiles = (
        lax.dynamic_slice_in_dim(row_tiles, row_index * block_slots, block_slots)
        - row_index * block_tiles
    )
    far_tiles = (
        lax.dynamic_slice_in_dim(row_tiles, column_index * block_slots, block_slots)
        - column_index * block_tiles
    )
    tiled = sep_inverse.reshape(block_tiles, TILE, block_tiles, TILE)
    picked = jnp.take(jnp.take(tiled, own_tiles, axis=0), far_tiles, axis=2)
    picked = picked.reshape(block_slots * TILE, block_slots * TILE)
    own_white = jnp.dot(
        panel_rows, diag_inverse, precision=highest, preferred_element_type=jnp.float32
    )
    far_white = broadcast(own_white, "row", column_index)
    partial_value = -jnp.dot(
        picked, far_white, precision=highest, preferred_element_type=jnp.float32
    )
    piece = partial_value.shape[0] // members
    count = width // members
    first = column_index * count
    sigma_rows = lax.psum_scatter(partial_value, ("col", "rep"), scatter_dimension=0, tiled=True)
    white_mine = lax.dynamic_slice_in_dim(own_white, column_index * piece, piece, 0)
    local_block = lax.psum_scatter(
        contract_rows(sigma_rows, white_mine), ("col", "rep"), scatter_dimension=0, tiled=True
    )
    summed = lax.psum(local_block, "row")
    inverse_cols = lax.dynamic_slice_in_dim(diag_inverse, first, count, 1)
    sigma_diag = contract_rows(inverse_cols, diag_inverse) - summed
    variances = jnp.diagonal(lax.dynamic_slice_in_dim(sigma_diag, first, count, 1))
    return (sigma_rows, sigma_diag, variances)


def split(x):
    high = x.astype(jnp.bfloat16)
    return high, (x - high.astype(jnp.float32)).astype(jnp.bfloat16)


def dot(a, b):
    return jnp.dot(a, b, preferred_element_type=jnp.float32)


def dot3(a, b):
    return dot(a[0], b[0]) + (dot(a[0], b[1]) + dot(a[1], b[0]))


def f32(*shape):
    return jax.ShapeDtypeStruct(shape, jnp.float32)


def first_kernel(
    tiles_hbm, sep_hbm, panel_hbm, inverse_hbm, white_hbm, picked_hbm, *scratch
):
    tiles, panel, inverse, white_ref, picked_ref, sems, out_sems = scratch
    row, member = lax.axis_index("row"), lax.axis_index(("col", "rep"))
    columns = pl.ds(pl.multiple_of(member * TILE, TILE), TILE)
    slots, block = picked_ref.shape[0] // TILE, sep_hbm.shape[0] // TILE
    fetch = [
        pltpu.make_async_copy(tiles_hbm, tiles, sems.at[0]),
        pltpu.make_async_copy(panel_hbm, panel, sems.at[1]),
        pltpu.make_async_copy(inverse_hbm.at[:, columns], inverse, sems.at[2]),
    ]
    for copy in fetch:
        copy.start()
    fetch[0].wait()
    picks = []
    for i in range(slots):
        down = (tiles[row * slots + i] - row * block) * TILE
        for j in range(slots):
            across = (tiles[member * slots + j] - member * block) * TILE
            picks.append(
                pltpu.make_async_copy(
                    sep_hbm.at[
                        pl.ds(pl.multiple_of(down, TILE), TILE),
                        pl.ds(pl.multiple_of(across, TILE), TILE),
                    ],
                    picked_ref.at[pl.ds(i * TILE, TILE), pl.ds(j * TILE, TILE)],
                    sems.at[3 + i * slots + j],
                )
            )
    for copy in picks:
        copy.start()
    fetch[1].wait()
    fetch[2].wait()
    high, low = split(panel[...])
    parts = split(inverse[...])
    wide = dot(high, jnp.concatenate(parts, axis=1))
    white_ref[...] = wide[:, :TILE] + (wide[:, TILE:] + dot(low, parts[0]))
    out = [pltpu.make_async_copy(white_ref, white_hbm, out_sems.at[0])]
    out[0].start()
    for i in range(slots):
        for copy in picks[i * slots : (i + 1) * slots]:
            copy.wait()
        rows = pl.ds(i * TILE, TILE)
        out.append(
            pltpu.make_async_copy(picked_ref.at[rows, :], picked_hbm.at[rows, :], out_sems.at[1 + i])
        )
        out[-1].start()
    for copy in out:
        copy.wait()


def first(row_tiles, sep_inverse, panel_rows, diag_inverse):
    slots = panel_rows.shape[0] // TILE
    return pl.pallas_call(
        first_kernel,
        out_shape=(f32(panel_rows.shape[0], TILE), f32(slots * TILE, slots * TILE)),
        in_specs=[ANY] * 4,
        out_specs=(ANY, ANY),
        scratch_shapes=[
            pltpu.SMEM(row_tiles.shape, jnp.int32),
            pltpu.VMEM(panel_rows.shape, jnp.float32),
            pltpu.VMEM((diag_inverse.shape[0], TILE), jnp.float32),
            pltpu.VMEM((panel_rows.shape[0], TILE), jnp.float32),
            pltpu.VMEM((slots * TILE, slots * TILE), jnp.float32),
            pltpu.SemaphoreType.DMA((3 + slots * slots,)),
            pltpu.SemaphoreType.DMA((1 + slots,)),
        ],
    )(row_tiles, sep_inverse, panel_rows, diag_inverse)


def whiten_kernel(*refs):
    panel_ref, inverse_ref, quarter_ref, own_ref, near_ref = refs[:5]
    high_ref, low_ref, base_ref, quarter_out, sep_high, sep_low = refs[5:]
    member = lax.axis_index(("col", "rep"))
    columns = pl.ds(pl.multiple_of(member * TILE, TILE), TILE)
    inverse = split(inverse_ref[...])
    high_ref[...], low_ref[...] = split(dot3(split(panel_ref[...]), inverse))
    base_ref[...] = dot3(split(inverse_ref[:, columns].T), inverse)
    quarter_out[:, :TILE], quarter_out[:, TILE:] = split(quarter_ref[...])
    depth = own_ref.shape[1]
    sep_high[:, :depth], sep_low[:, :depth] = split(own_ref[...])
    sep_high[:, depth:], sep_low[:, depth:] = split(near_ref[...])


def whiten(panel_rows, diag_inverse, quarter, own, near):
    def part(*shape):
        return jax.ShapeDtypeStruct(shape, jnp.bfloat16)

    white, sep = part(*panel_rows.shape), part(own.shape[0], 2 * own.shape[1])
    out = pl.pallas_call(
        whiten_kernel,
        out_shape=(
            white,
            white,
            f32(TILE, diag_inverse.shape[1]),
            part(quarter.shape[0], 2 * TILE),
            *[sep] * 2,
        ),
        in_specs=[VMEM] * 5,
        out_specs=(VMEM,) * 6,
        compiler_params=PARAMS,
    )(panel_rows, diag_inverse, quarter, own, near)
    return out[:2], out[2], out[3], out[4:]


def product_kernel(*refs):
    base, sep_high, sep_low, across, quarter, *far = refs[:-15]
    whites, (white_high, white_low) = refs[-15:-12], refs[-12:-10]
    terms, pieces, (joined, product, other_high, other_low) = refs[-10:-6], refs[-6:-4], refs[-4:]
    row, member = lax.axis_index("row"), lax.axis_index(("col", "rep"))
    depth = across.shape[1]

    def place(j):
        return pl.ds(pl.multiple_of((row ^ j ^ member) * depth, TILE), depth)

    joined[place(0), :] = quarter[...]
    for j, ref in zip(ORDER, whites):
        joined[place(j), :TILE], joined[place(j), TILE:] = split(ref[...])
    other_high[:, :depth], other_low[:, :depth] = split(across[...])
    count = far[0].shape[0]
    for n, ref in enumerate(far):
        rows = slice(n * count, (n + 1) * count)
        other_high[rows, depth:], other_low[rows, depth:] = split(ref[...])
    wide = dot(sep_high[...], joined[: 2 * depth, :]) + dot(other_high[...], joined[2 * depth :, :])
    low = dot(sep_low[...], joined[: 2 * depth, :TILE]) + dot(other_low[...], joined[2 * depth :, :TILE])
    total = wide[:, :TILE] + (wide[:, TILE:] + low)
    product[...] = -total
    flipped = split(total.T)
    stacked = jnp.concatenate(flipped)
    depth = pieces[0].shape[0] // 2
    both = dot(stacked, white_high[...])
    full = both[:TILE] + (both[TILE:] + dot(flipped[0], white_low[...]))
    for j in range(4):
        value = full[:, :TILE]
        for n in range(1, 4):
            value = jnp.where((row ^ j) == n, full[:, n * TILE : (n + 1) * TILE], value)
        if j == 0:
            value += base[:, pl.ds(pl.multiple_of(row * TILE, TILE), TILE)]
        terms[j][...] = value
        mine = pl.ds(pl.multiple_of((member ^ j) * depth, 8), depth)
        pieces[j % 2][j // 2 * depth : (j // 2 + 1) * depth, :] = product[mine, :]


def products(base, seps, across, quarter, far, whites, own_white):
    depth, width = whites[0].shape
    return pl.pallas_call(
        product_kernel,
        out_shape=(f32(width, TILE),) * 4 + (f32(depth // 2, width),) * 2,
        in_specs=[VMEM] * (10 + len(far)),
        out_specs=(VMEM,) * 6,
        scratch_shapes=[
            pltpu.VMEM((4 * depth, 2 * width), jnp.bfloat16),
            pltpu.VMEM((depth, width), jnp.float32),
            pltpu.VMEM((depth, 2 * depth), jnp.bfloat16),
            pltpu.VMEM((depth, 2 * depth), jnp.bfloat16),
        ],
        compiler_params=PARAMS,
    )(base, *seps, across, quarter, *far, *whites, *own_white)


def rows_kernel(own, near, across, far, out_ref):
    member, count = lax.axis_index(("col", "rep")), out_ref.shape[0]
    blocks = (own[:count, :], near[:count, :], across[...], far[...])
    for j, block in enumerate(blocks):
        out_ref[:, pl.ds(pl.multiple_of((member ^ j) * TILE, TILE), TILE)] = block


def rows_of(own, near, across, far):
    count, width = own.shape
    return pl.pallas_call(
        rows_kernel,
        out_shape=f32(count // 2, 4 * width),
        in_specs=[VMEM] * 4,
        out_specs=VMEM,
        compiler_params=PARAMS,
    )(own, near, across, far)


def diagonal_kernel(own, first, second, third, out_ref, variances_ref):
    row, member = lax.axis_index("row"), lax.axis_index(("col", "rep"))
    for j, ref in zip((0,) + ORDER, (own, first, second, third)):
        columns = pl.ds(pl.multiple_of((row ^ j) * TILE, TILE), TILE)
        out_ref[:, columns] = ref[...]
    square = out_ref[:, pl.ds(pl.multiple_of(member * TILE, TILE), TILE)]
    across = lax.broadcasted_iota(jnp.int32, square.shape, 0)
    down = lax.broadcasted_iota(jnp.int32, square.shape, 1)
    variances_ref[...] = jnp.sum(jnp.where(across == down, square, 0.0), axis=0, keepdims=True)


def diagonal(blocks):
    return pl.pallas_call(
        diagonal_kernel,
        out_shape=(f32(TILE, 4 * TILE), f32(1, TILE)),
        in_specs=[VMEM] * 4,
        out_specs=(VMEM, VMEM),
        compiler_params=PARAMS,
    )(*blocks)


def rows_apart(j):
    return [(i, i ^ j) for i in range(4)]


SWAP = [(0, 1), (1, 0)]


def four_by_four(sep_inverse, row_tiles, panel_rows, diag_inverse):
    quarter, own = first(row_tiles, sep_inverse, panel_rows, diag_inverse)
    across = lax.ppermute(own, "col", SWAP)
    near = lax.ppermute(own, "rep", SWAP)
    whites = {j: lax.ppermute(quarter, "row", rows_apart(j)) for j in (3, 1)}
    whites[2] = lax.ppermute(whites[3], "row", rows_apart(1))
    own_white, base, split_quarter, seps = whiten(panel_rows, diag_inverse, quarter, own, near)
    across, own_white, base = lax.optimization_barrier((across, own_white, base))
    count = across.shape[0] // 3
    far = [
        lax.ppermute(lax.slice_in_dim(across, i * count, (i + 1) * count), "rep", SWAP)
        for i in range(3)
    ]
    out = products(base, seps, across, split_quarter, far, [whites[j] for j in ORDER], own_white)
    terms, (mine, others) = out[:4], out[4:]
    near = lax.ppermute(others, "rep", SWAP)
    got = [lax.ppermute(terms[j], "row", rows_apart(j)) for j in (2, 1, 3)]
    count = mine.shape[0] // 2
    across = lax.ppermute(mine[count:], "col", SWAP)
    far = lax.ppermute(near[count:], "col", SWAP)
    block = terms[0] + got[0] + got[1] + got[2]
    again, across, far = lax.optimization_barrier((block, across, far))
    sent = zip(ORDER, (block, block, again))
    blocks = [block] + [lax.ppermute(x, "row", rows_apart(j)) for j, x in sent]
    sigma_rows = rows_of(mine, near, across, far)
    blocks, sigma_rows = lax.optimization_barrier((blocks, sigma_rows))
    sigma_diag, variances = diagonal(blocks)
    return sigma_rows, sigma_diag, variances.reshape(-1)


def solution(mesh):
    shape = mesh.shape

    def per_device(sep_inverse, row_tiles, panel_rows, diag_inverse):
        square = (shape["row"], shape["col"], shape["rep"]) == (4, 2, 2)
        fits = diag_inverse.shape == (4 * TILE, 4 * TILE) and panel_rows.shape[0] % (3 * TILE) == 0
        form = four_by_four if square and fits else any_mesh
        return form(sep_inverse, row_tiles, panel_rows, diag_inverse)

    return jax.shard_map(
        per_device,
        mesh=mesh,
        in_specs=(
            P(("groups", "row"), ("col", "rep")),
            P(),
            P(("groups", "row"), None),
            P("groups", None),
        ),
        out_specs=(
            P(("groups", "row", "col", "rep"), None),
            P(("groups", "col", "rep"), None),
            P(("groups", "col", "rep")),
        ),
        check_vma=False,
    )
```
